256 devices in a mesh: row: 4 (over x), tm: 64 (over z, y, core).
Axes of the slice: x: 4, y: 4, z: 8, core: 2. Of those that a mesh axis runs over, the one named last changes fastest.
Arguments:
- snapshots: bfloat16 [64, 2048, 2048], P('tm', 'row'), may hold values from -10 to 10
- basis: bfloat16 [64, 2048, 64], P('tm', 'row'), may hold values from -0.125 to 0.125
- neighbour_ids: int32 [64, 2], replicated, may hold values from 0 to 63, as said below
Outputs:
- feature_gram: float32 [64, 2272, 2272], P('tm', 'row')
The draws below stay inside these ranges and needn't reach their ends.
Inputs may be any that keep to these rules, and one draw needn't show every extreme that they name: `neighbour_ids`: row s is coupled to subdomain s - 1 (cyclically, around the annulus) in its first entry, and in its second to another subdomain that is neither s nor s - 1.
All inputs are finite; a program needn't handle non-finite values.
Results may differ from the reference program's by a relative error of at most 0.005.
Values may be sent and summed in bfloat16 or wider, within the bound.
A program may use at most 64 MiB of HBM per device.

```python
import jax
import jax.numpy as jnp
import numpy as np
from jax import lax

R = 64
NB = 2
SUB = 64
CELLS = 2048
TIME = 2048


def draw_snapshots(key, part):
    key = jax.random.fold_in(key, 11)
    key_main, key_rough = jax.random.split(key, 2)
    ramp = jnp.arange(TIME, dtype=jnp.float32) / (TIME - 1)
    rough = jax.random.uniform(key_rough, (TIME,), jnp.float32, 0.6, 1.4)
    amplitude = 3.0 ** (0.5 * ramp) * rough
    values = jnp.clip(jax.random.normal(key_main, (SUB, CELLS, TIME), jnp.float32), -4.0, 4.0) * amplitude
    return values.astype(jnp.bfloat16)


def draw_neighbour_ids(key, part):
    key = jax.random.fold_in(key, 23)
    owners = jnp.arange(SUB, dtype=jnp.int32)
    first = (owners + SUB - 1) % SUB
    offset = jax.random.randint(key, (SUB,), 0, SUB - 2, dtype=jnp.int32)
    second = (owners + 1 + offset) % SUB
    return jnp.stack([first, second], axis=1).astype(jnp.int32)


def shard_levels(key, extent, shards, smallest, high):
    def one(dim, blocks):
        heights = jax.random.uniform(jax.random.fold_in(jax.random.fold_in(key, 6), dim), (blocks,), jnp.float32, smallest / len(shards), high / len(shards))
        return jnp.repeat(jnp.exp(heights), extent[dim] // blocks).reshape((-1,) + (1,) * (len(extent) - dim - 1))

    factor_of = one(*shards[0])
    for cut in shards[1:]:
        factor_of = factor_of * one(*cut)
    return factor_of


def bell_draw(rng, shape, spread, limit, cuts=(), held_as=jnp.bfloat16):
    level = shard_levels(rng, shape, cuts, -0.22, 0.18) if cuts else 1.0
    values = jax.random.normal(rng, shape, jnp.float32) * spread * level
    return jnp.minimum(jnp.maximum(values, -limit), limit).astype(held_as)


def setup_inputs(seed: int = 0) -> dict:
    arg_keys = jax.random.split(jax.random.key(seed), 4)
    snapshots = draw_snapshots(jax.random.fold_in(arg_keys[3], 71), 0)
    basis = bell_draw(arg_keys[1], (SUB, CELLS, R), CELLS ** -0.5, 0.125, ((0, 64), (1, 4)))
    neighbour_ids = draw_neighbour_ids(jax.random.fold_in(arg_keys[3], 71), 0)
    return dict(snapshots=snapshots, basis=basis, neighbour_ids=neighbour_ids)


def reference(snapshots, basis, neighbour_ids):
    upper_i, upper_j = np.triu_indices(R)

    def project(pair):
        data, columns = pair
        coords = jnp.dot(data.T, columns, preferred_element_type=jnp.float32)
        energy = lax.optimization_barrier(jnp.sum(coords * coords, axis=0))
        scale = lax.rsqrt(energy / TIME + 1e-06)
        return (coords * scale).astype(jnp.bfloat16)
    normed = lax.map(project, (snapshots, basis))

    def gram(index):
        own = normed[index]
        parts = [own]
        for slot in range(NB):
            parts.append(normed[neighbour_ids[index, slot]])
        quad = (own[:, upper_i].astype(jnp.float32) * own[:, upper_j].astype(jnp.float32)).astype(jnp.bfloat16)
        features = jnp.concatenate(parts + [quad], axis=1)
        return jnp.dot(features.T, features, preferred_element_type=jnp.float32) / TIME
    return lax.map(gram, jnp.arange(SUB, dtype=jnp.int32))
```

```python
import jax
import jax.numpy as jnp
import numpy as np
from jax import lax
from jax.experimental import pallas as pl
from jax.experimental.pallas import tpu as pltpu
from jax.sharding import PartitionSpec as P

MESH = pl.DeviceIdType.MESH
BF = jnp.bfloat16
F32 = jnp.float32


def place():
    t = lax.axis_index("tm")
    return lax.axis_index("row"), lax.div(t, 8), lax.rem(lax.div(t, 2), 4), lax.rem(t, 2)


def at(x, z, y, c):
    return (lax.rem(x, 4), (lax.rem(z, 8) * 4 + lax.rem(y, 4)) * 2 + lax.rem(c, 2))


def comm_kernel(snap, basis, ids, own, n1, n2, sv, psend, precv, gath, zsend, zrecv,
                ld, ps, pr, os, orr, ys, yr, cs, cr, ns, nr, n1s, n1r, zs, zr, n2s, n2r):
    x, z, y, c = place()
    s = lax.axis_index("tm")
    s_next = (lax.axis_index("row"), lax.rem(s + 1, 64))
    s_prev = (lax.axis_index("row"), lax.rem(s + 63, 64))

    def cols(q):
        return pl.ds(pl.multiple_of(q * 512, 512), 512)

    def remote(src, dst, ss, rs, dev):
        return pltpu.make_async_remote_copy(src_ref=src, dst_ref=dst, send_sem=ss, recv_sem=rs,
                                            device_id=dev, device_id_type=MESH)

    quarter = [lax.rem(x + k, 4) for k in (1, 2, 3, 0)]
    loads = [pltpu.make_async_copy(snap.at[:, cols(q)], sv.at[:, cols(q)], ld.at[i]) for i, q in enumerate(quarter)]
    for cp in loads:
        cp.start()

    bar = pltpu.get_barrier_semaphore()
    peers = [at(x + k, z, y, c) for k in (1, 2, 3)] + [at(x, z, y + k, c) for k in (1, 2, 3)]
    peers += [at(x, z + k, y, c) for k in range(1, 8)] + [at(x, z, y, c + 1), s_next, s_prev]
    for p in peers:
        pl.semaphore_signal(bar, inc=1, device_id=p, device_id_type=MESH)

    def project(i):
        loads[i].wait()
        return lax.dot_general(basis[...], sv[:, cols(quarter[i])], (((0,), (0,)), ((), ())), preferred_element_type=F32)

    sums = []
    for i in range(3):
        psend[i] = project(i).astype(BF)
        if i == 0:
            pl.semaphore_wait(bar, len(peers))
        cp = remote(psend.at[i], precv.at[i], ps.at[i], pr.at[i], at(x + i + 1, z, y, c))
        cp.start()
        sums.append(cp)
    total = project(3)
    for i in range(3):
        sums[i].wait_recv()
        total = total + precv[i].astype(F32)

    me = y * 2 + c
    gath[me] = total.astype(BF)
    own[x] = total
    ycp, ccp = [], []
    for k in (1, 2, 3):
        cp = remote(gath.at[me], gath.at[me], ys.at[k - 1], yr.at[k - 1], at(x, z, y + k, c))
        cp.start()
        ycp.append(cp)
    cp = remote(gath.at[me], gath.at[me], cs.at[0], cr.at[0], at(x, z, y, c + 1))
    cp.start()
    ccp.append(cp)
    ncp = remote(gath.at[me], n1.at[x], ns.at[0], nr.at[0], s_next)
    ncp.start()
    ocp = []
    for k in (1, 2, 3):
        cp = remote(own.at[x], own.at[x], os.at[k - 1], orr.at[k - 1], at(x + k, z, y, c))
        cp.start()
        ocp.append(cp)

    for k in (1, 3, 2):
        ycp[k - 1].wait_recv()
        slot = lax.rem(y + 4 - k, 4) * 2 + c
        cp = remote(gath.at[slot], gath.at[slot], cs.at[k], cr.at[k], at(x, z, y, c + 1))
        cp.start()
        ccp.append(cp)
    ncp.wait_recv()
    n1cp = []
    for k in (1, 2, 3):
        cp = remote(n1.at[x], n1.at[x], n1s.at[k - 1], n1r.at[k - 1], at(x + k, z, y, c))
        cp.start()
        n1cp.append(cp)
    for cp in ccp:
        cp.wait_recv()
    zcp = []
    for k in (4, 3, 5, 2, 6, 1, 7):
        owner = (lax.rem(z + k, 8) * 4 + y) * 2 + c
        zsend[k - 1] = gath[lax.rem(ids[owner, 1], 8)]
        cp = remote(zsend.at[k - 1], zrecv.at[z], zs.at[k - 1], zr.at[k - 1], at(x, z + k, y, c))
        cp.start()
        zcp.append(cp)
    want = ids[s, 1]
    zrecv[z] = gath[lax.rem(want, 8)]
    for cp in zcp:
        cp.wait_recv()
    n2[x] = zrecv[lax.div(want, 8)]
    n2cp = []
    for k in (1, 2, 3):
        cp = remote(n2.at[x], n2.at[x], n2s.at[k - 1], n2r.at[k - 1], at(x + k, z, y, c))
        cp.start()
        n2cp.append(cp)
    for cp in ocp + n1cp + n2cp:
        cp.wait_recv()
    for cp in sums + ycp + ccp + [ncp] + ocp + n1cp + zcp + n2cp:
        cp.wait_send()


def comm_call(snap, basis, ids):
    vm = pl.BlockSpec(memory_space=pltpu.VMEM)
    dma = pltpu.SemaphoreType.DMA
    sems = [4, 3, 3, 3, 3, 3, 3, 4, 4, 1, 1, 3, 3, 7, 7, 3, 3]
    return pl.pallas_call(
        comm_kernel,
        out_shape=[jax.ShapeDtypeStruct((4, 64, 512), d) for d in (F32, BF, BF)],
        in_specs=[pl.BlockSpec(memory_space=pl.ANY), vm, pl.BlockSpec(memory_space=pltpu.SMEM)],
        out_specs=[vm] * 3,
        scratch_shapes=[pltpu.VMEM((512, 2048), BF), pltpu.VMEM((3, 64, 512), BF), pltpu.VMEM((3, 64, 512), BF),
                        pltpu.VMEM((8, 64, 512), BF), pltpu.VMEM((7, 64, 512), BF), pltpu.VMEM((8, 64, 512), BF)]
        + [dma((n,)) for n in sems],
        compiler_params=pltpu.CompilerParams(collective_id=0, has_side_effects=True, vmem_limit_bytes=40 * 2**20),
        name="exchange",
    )(snap, basis, ids)

RANK=64
PAD=8
TRI=[(i,j) for i in range(RANK) for j in range(i,RANK)]

def quad_tile(nf, c, q0, sub):
    out=None
    q=q0
    while q < q0+8:
        i,j=TRI[q]
        run=min(RANK-j, q0+8-q)
        b=q-q0
        val = nf[c, pl.ds(PAD+i,1), :] * nf[c, pl.ds(PAD+j-b, 8), :]
        out = val if out is None else jnp.where(sub < b, out, val)
        q+=run
    return out

def build_own(own, nf, F):
    T=2048
    e=None
    for r in range(4):
        v=own[r]; s=jnp.sum(v*v,axis=1,keepdims=True); e = s if e is None else e+s
    sc=lax.rsqrt(e/T+1e-6)
    for r in range(4):
        n=(own[r]*sc).astype(jnp.bfloat16)
        F[0:64, pl.ds(512*r,512)] = n
        nn=n.astype(jnp.float32)
        for k in range(4):
            nf[4*r+k, pl.ds(PAD,64), :] = nn[:, 128*k:128*k+128]

def build_nb(nb, row, F):
    T=2048
    e=None
    for r in range(4):
        v=nb[r].astype(jnp.float32); s=jnp.sum(v*v,axis=1,keepdims=True); e = s if e is None else e+s
    sc=lax.rsqrt(e/T+1e-6)
    for r in range(4):
        F[row:row+64, pl.ds(512*r,512)] = (nb[r].astype(jnp.float32)*sc).astype(jnp.bfloat16)

def build_quads(nf, F):
    sub=lax.broadcasted_iota(jnp.int32,(8,128),0)
    def chunk(c,_):
        col=pl.ds(pl.multiple_of(c*128,128),128)
        for t in range(0,len(TRI),16):
            a=quad_tile(nf,c,t,sub); b=quad_tile(nf,c,t+8,sub)
            F[192+t:192+t+16, col] = jnp.concatenate([a,b],0).astype(jnp.bfloat16)
        return 0
    lax.fori_loop(0,16,chunk,0)

def gram_kernel(own, n1, n2, o, F, nf, acc):
    j=pl.program_id(0)
    x=lax.axis_index("row")
    @pl.when(j==0)
    def _():
        nf[:, 0:PAD, :] = jnp.zeros((16,PAD,128),jnp.float32)
        nf[:, PAD+64:PAD+72, :] = jnp.zeros((16,8,128),jnp.float32)
        F[2272:2304,:]=jnp.zeros((32,2048),jnp.bfloat16)
        build_own(own,nf,F); build_nb(n1,64,F); build_nb(n2,128,F)
        build_quads(nf,F)
    rs=pl.multiple_of((x*568)//16*16,16)
    ofs=pl.multiple_of((x%2)*8,8)
    lhs=F[pl.ds(rs,576),:]
    rhs=F[pl.ds(pl.multiple_of(j*256,256),256),:]
    acc[...]=lax.dot_general(lhs,rhs,(((1,),(1,)),((),())),preferred_element_type=jnp.float32)
    o[...]=acc[pl.ds(ofs,568),:]*(1.0/2048)

def gram_call(own,n1,n2):
    return pl.pallas_call(gram_kernel, grid=(9,),
        out_shape=jax.ShapeDtypeStruct((568,2272),jnp.float32),
        in_specs=[pl.BlockSpec((4,64,512),lambda j:(0,0,0))]*3,
        out_specs=pl.BlockSpec((568,256),lambda j:(0,j)),
        scratch_shapes=[pltpu.VMEM((2304,2048),jnp.bfloat16), pltpu.VMEM((16,PAD+72,128),jnp.float32), pltpu.VMEM((576,256),jnp.float32)],
        compiler_params=pltpu.CompilerParams(vmem_limit_bytes=60*2**20, dimension_semantics=("arbitrary",)), name="gram")(own,n1,n2)


def on_device(snapshots, basis, neighbour_ids):
    own, n1, n2 = comm_call(snapshots[0], basis[0], neighbour_ids)
    return gram_call(own, n1, n2)[None]


def solution(mesh):
    return jax.shard_map(
        on_device,
        mesh=mesh,
        in_specs=(P("tm", "row", None), P("tm", "row", None), P()),
        out_specs=P("tm", "row", None),
        check_vma=False,
    )
```

```python
import jax
import jax.numpy as jnp
import numpy as np
from jax import lax
from jax.experimental import pallas as pl
from jax.experimental.pallas import tpu as pltpu
from jax.sharding import PartitionSpec as P

MESH = pl.DeviceIdType.MESH
BF = jnp.bfloat16
F32 = jnp.float32
RANK = 64
TIME = 2048
EPS = 1e-6
PAIRS = [(i, j) for i in range(RANK) for j in range(i, RANK)]
ROWS = 568
COLS = 2272
PAD = 8
NT = (((1,), (1,)), ((), ()))


def place():
    t = lax.axis_index("tm")
    return lax.axis_index("row"), lax.div(t, 8), lax.rem(lax.div(t, 2), 4), lax.rem(t, 2)


def at(x, z, y, c):
    return (lax.rem(x, 4), (lax.rem(z, 8) * 4 + lax.rem(y, 4)) * 2 + lax.rem(c, 2))


def remote(src, dst, ss, rs, dev):
    return pltpu.make_async_remote_copy(
        src_ref=src, dst_ref=dst, send_sem=ss, recv_sem=rs, device_id=dev, device_id_type=MESH
    )


def scale_of(blocks):
    energy = None
    for v in blocks:
        e = jnp.sum(v * v, axis=1, keepdims=True)
        energy = e if energy is None else energy + e
    return lax.rsqrt(energy / TIME + EPS)


def quad_tile(nf, chunk, first, line):
    out, q = None, first
    while q < first + 8:
        i, j = PAIRS[q]
        b = q - first
        val = nf[chunk, pl.ds(PAD + i, 1), :] * nf[chunk, pl.ds(PAD + j - b, 8), :]
        out = val if out is None else jnp.where(line < b, out, val)
        q += min(RANK - j, first + 8 - q)
    return out


def build_quads(nf, feats):
    line = lax.broadcasted_iota(jnp.int32, (8, 128), 0)

    def one(chunk, carry):
        col = pl.ds(pl.multiple_of(chunk * 128, 128), 128)
        for t in range(0, len(PAIRS), 16):
            pair = [quad_tile(nf, chunk, t, line), quad_tile(nf, chunk, t + 8, line)]
            feats[192 + t : 208 + t, col] = jnp.concatenate(pair, 0).astype(BF)
        return carry

    lax.fori_loop(0, TIME // 128, one, 0)


def exchange(snap, basis, ids_hbm, feats, gram,
             sv, bv, ids, psend, precv, own, raw, nf, gy, gz, zsend, zrecv, mix, msend, ysend, yrecv, n1, n2,
             ld, ps, pr, os, orr, ys, yr, cs, cr, gs, gr, ns, nr, n1s, n1r, zs, zr, ms, mr, qs, qr, n2s, n2r):
    x, z, y, c = place()
    s = lax.axis_index("tm")
    me = y * 2 + c
    s_next = (x, lax.rem(s + 1, 64))
    s_prev = (x, lax.rem(s + 63, 64))

    def cols(q):
        return pl.ds(pl.multiple_of(q * 512, 512), 512)

    order = (2, 1, 3, 0)
    quarter = [lax.rem(x + k, 4) for k in order]
    fetch = [pltpu.make_async_copy(basis, bv, ld.at[4]), pltpu.make_async_copy(ids_hbm, ids, ld.at[5])]
    loads = [pltpu.make_async_copy(snap.at[:, cols(q)], sv.at[:, cols(q)], ld.at[i]) for i, q in enumerate(quarter)]
    fetch[0].start()
    for cp in loads:
        cp.start()
    fetch[1].start()

    bar = pltpu.get_barrier_semaphore()
    peers = [at(x + k, z, y, c) for k in (1, 2, 3)] + [at(x, z, y + k, c) for k in (1, 2, 3)]
    peers += [at(x, z + k, y, c) for k in range(1, 8)] + [at(x, z, y, c + 1), s_next, s_prev]
    for p in peers:
        pl.semaphore_signal(bar, inc=1, device_id=p, device_id_type=MESH)

    def project(i):
        loads[i].wait()
        return jnp.dot(bv[...], sv[:, cols(quarter[i])], preferred_element_type=F32)

    fetch[0].wait()
    sums = []
    for i, k in enumerate(order[:3]):
        psend[i] = project(i).astype(BF)
        if i == 0:
            pl.semaphore_wait(bar, len(peers))
        cp = remote(psend.at[i], precv.at[i], ps.at[i], pr.at[i], at(x + k, z, y, c))
        cp.start()
        sums.append(cp)
    total = project(3)
    fetch[1].wait()
    feats[128:192, :] = jnp.zeros((64, TIME), BF)
    feats[COLS:, :] = jnp.zeros((feats.shape[0] - COLS, TIME), BF)
    nf[:, 0:PAD, :] = jnp.zeros((16, PAD, 128), F32)
    nf[:, PAD + RANK :, :] = jnp.zeros((16, 8, 128), F32)
    for i in range(3):
        sums[i].wait_recv()
        total = total + precv[i].astype(F32)

    own[x] = total
    low = total.astype(BF)
    gy[me] = low[:, :256]
    gz[z] = low[:, 256:]
    raw[...] = low
    ycp = {}
    for k in (2, 1, 3):
        ycp[k] = remote(gy.at[me], gy.at[me], ys.at[k - 1], yr.at[k - 1], at(x, z, y + k, c))
        ycp[k].start()
    ccp = [remote(gy.at[me], gy.at[me], cs.at[0], cr.at[0], at(x, z, y, c + 1))]
    ccp[0].start()
    gcp = {}
    for k in (4, 3, 5, 2, 6, 1, 7):
        gcp[k] = remote(gz.at[z], gz.at[z], gs.at[k - 1], gr.at[k - 1], at(x, z + k, y, c))
        gcp[k].start()
    ncp = remote(raw, n1.at[x], ns.at[0], nr.at[0], s_next)
    ncp.start()
    ocp = []
    for k in (2, 1, 3):
        cp = remote(own.at[x], own.at[x], os.at[k - 1], orr.at[k - 1], at(x + k, z, y, c))
        cp.start()
        ocp.append(cp)

    for k in (1, 3, 2):
        ycp[k].wait_recv()
        slot = lax.rem(y + 4 - k, 4) * 2 + c
        cp = remote(gy.at[slot], gy.at[slot], cs.at[k], cr.at[k], at(x, z, y, c + 1))
        cp.start()
        ccp.append(cp)
    for cp in ccp:
        cp.wait_recv()
    want = ids[1, s]
    zcp = {}
    for k in (4, 3, 5, 2, 6, 1, 7):
        asked = ids[1, (lax.rem(z + k, 8) * 4 + y) * 2 + c]
        zsend[k - 1] = gy[lax.rem(asked, 8)]
        zcp[k] = remote(zsend.at[k - 1], zrecv.at[z], zs.at[k - 1], zr.at[k - 1], at(x, z + k, y, c))
        zcp[k].start()
    zrecv[z] = gy[lax.rem(want, 8)]

    ncp.wait_recv()
    n1cp = []
    for k in (2, 1, 3):
        cp = remote(n1.at[x], n1.at[x], n1s.at[k - 1], n1r.at[k - 1], at(x + k, z, y, c))
        cp.start()
        n1cp.append(cp)

    for k in (1, 7, 2, 6, 3, 5, 4):
        gcp[k].wait_recv()
    for yy in range(4):
        msend[yy] = gz[lax.div(ids[1, (z * 4 + yy) * 2 + 1 - c], 8)]
    mcp = remote(msend, mix.at[c], ms.at[0], mr.at[0], at(x, z, y, c + 1))
    mcp.start()
    for yy in range(4):
        mix[c, yy] = gz[lax.div(ids[1, (z * 4 + yy) * 2 + c], 8)]

    for cp in ocp:
        cp.wait_recv()
    scale = scale_of([own[r] for r in range(4)])
    for r in range(4):
        n = (own[r] * scale).astype(BF)
        feats[0:64, 512 * r : 512 * r + 512] = n
        wide = n.astype(F32)
        for k in range(4):
            nf[4 * r + k, pl.ds(PAD, RANK), :] = wide[:, 128 * k : 128 * k + 128]

    mcp.wait_recv()
    qcp = []
    for k in (2, 1, 3):
        yy = lax.rem(y + k, 4)
        asked = ids[1, (z * 4 + yy) * 2 + c]
        ysend[k - 1] = mix[lax.rem(asked, 2), yy]
        cp = remote(ysend.at[k - 1], yrecv.at[y], qs.at[k - 1], qr.at[k - 1], at(x, z, y + k, c))
        cp.start()
        qcp.append(cp)
    yrecv[y] = mix[lax.rem(want, 2), y]

    def neighbour(ref, row):
        blocks = [ref[r].astype(F32) for r in range(4)]
        scale = scale_of(blocks)
        for r in range(4):
            feats[row : row + 64, 512 * r : 512 * r + 512] = (blocks[r] * scale).astype(BF)

    for cp in n1cp:
        cp.wait_recv()
    neighbour(n1, 64)
    build_quads(nf, feats)

    n2cp = []

    def share(h):
        for k in (2, 1, 3):
            sem = 3 * h + k - 1
            cp = remote(n2.at[h, x], n2.at[h, x], n2s.at[sem], n2r.at[sem], at(x + k, z, y, c))
            cp.start()
            n2cp.append(cp)

    for cp in qcp:
        cp.wait_recv()
    n2[1, x] = yrecv[lax.div(lax.rem(want, 8), 2)]
    share(1)
    for k in (1, 7, 2, 6, 3, 5, 4):
        zcp[k].wait_recv()
    n2[0, x] = zrecv[lax.div(want, 8)]
    share(0)

    start = pl.multiple_of(lax.div(x * ROWS, 16) * 16, 16)
    lines = pl.ds(start, 576)
    for lo, hi in [(0, 128)] + [(k, min(k + 256, COLS)) for k in range(256, COLS, 256)]:
        top = min(lo + 256, feats.shape[0]) if lo else 128
        block = lax.dot_general(feats[lines, :], feats[lo:top, :], NT, preferred_element_type=F32)
        gram[:, lo:hi] = block[:, : hi - lo] * (1.0 / TIME)

    for cp in n2cp:
        cp.wait_recv()
    halves = [n2[h, r].astype(F32) for r in range(4) for h in range(2)]
    scale = scale_of(halves)
    for r in range(8):
        feats[128:192, 256 * r : 256 * r + 256] = (halves[r] * scale).astype(BF)
    for cp in sums + list(ycp.values()) + ccp + list(gcp.values()) + [ncp] + ocp + n1cp + list(zcp.values()) + [mcp] + qcp + n2cp:
        cp.wait_send()


def exchange_call(snap, basis, ids):
    vm = pl.BlockSpec(memory_space=pltpu.VMEM)
    hbm = pl.BlockSpec(memory_space=pltpu.HBM)
    dma = pltpu.SemaphoreType.DMA
    half = (64, 256)
    full = (64, 512)
    sems = [6, 3, 3, 3, 3, 3, 3, 4, 4, 7, 7, 1, 1, 3, 3, 7, 7, 1, 1, 3, 3, 6, 6]
    bufs = [(512, 2048), (64, 512), None, (3,) + full, (3,) + full, (4,) + full, full, (16, PAD + RANK + 8, 128),
            (8,) + half, (8,) + half, (7,) + half, (8,) + half, (2, 4) + half, (4,) + half, (3,) + half, (4,) + half,
            (4,) + full, (2, 4) + half]
    wide = (5, 7)
    scratch = [pltpu.SMEM((2, 64), jnp.int32) if b is None else pltpu.VMEM(b, F32 if i in wide else BF) for i, b in enumerate(bufs)]
    return pl.pallas_call(
        exchange,
        out_shape=[jax.ShapeDtypeStruct((2304, TIME), BF), jax.ShapeDtypeStruct((576, COLS), F32)],
        in_specs=[hbm] * 3,
        out_specs=[vm] * 2,
        scratch_shapes=scratch + [dma((n,)) for n in sems],
        compiler_params=pltpu.CompilerParams(collective_id=0, has_side_effects=True, vmem_limit_bytes=24 * 2**20),
        name="exchange",
    )(snap, basis, ids)


def finish(feats, gram, out, mid, rows, sem):
    x = lax.axis_index("row")
    off = pl.multiple_of(lax.rem(x, 2) * 8, 8)
    spans = [(0, 128), (256, COLS)]

    def ship(src, lo, hi, cl, ch, n):
        return pltpu.make_async_copy(src, out.at[pl.ds(lo, hi - lo), pl.ds(cl, ch - cl)], sem.at[n])

    early = []
    for n, (cl, ch) in enumerate(spans):
        for m, (lo, hi) in enumerate([(0, 128), (192, ROWS)]):
            early.append(ship(gram.at[pl.ds(off + lo, hi - lo), pl.ds(cl, ch - cl)], lo, hi, cl, ch, 2 * n + m))
    for cp in early:
        cp.start()
    middle = [ship(gram.at[pl.ds(off + 128, 64), pl.ds(cl, ch - cl)], 128, 192, cl, ch, 4 + n) for n, (cl, ch) in enumerate(spans)]
    late = [ship(rows.at[:, pl.ds(cl, ch - cl)], 128, 192, cl, ch, 4 + n) for n, (cl, ch) in enumerate(spans)]

    @pl.when(x != 0)
    def _():
        for cp in middle:
            cp.start()

    lines = pl.ds(pl.multiple_of(lax.div(x * ROWS, 16) * 16, 16), 576)
    mid[...] = lax.dot_general(feats[lines, :], feats[128:256, :], NT, preferred_element_type=F32) * (1.0 / TIME)
    centre = ship(mid.at[pl.ds(off, ROWS), :], 0, ROWS, 128, 256, 6)
    centre.start()

    @pl.when(x == 0)
    def _():
        for lo in range(0, COLS, 256):
            hi = min(lo + 256, COLS)
            block = lax.dot_general(feats[128:192, :], feats[lo : lo + 256, :], NT, preferred_element_type=F32)
            rows[:, lo:hi] = block[:, : hi - lo] * (1.0 / TIME)
        for cp in late:
            cp.start()

    for cp in early + middle + [centre]:
        cp.wait()


def finish_call(feats, gram):
    vm = pl.BlockSpec(memory_space=pltpu.VMEM)
    return pl.pallas_call(
        finish,
        out_shape=jax.ShapeDtypeStruct((ROWS, COLS), F32),
        in_specs=[vm] * 2,
        out_specs=pl.BlockSpec(memory_space=pltpu.HBM),
        scratch_shapes=[pltpu.VMEM((576, 128), F32), pltpu.VMEM((64, COLS), F32), pltpu.SemaphoreType.DMA((7,))],
        compiler_params=pltpu.CompilerParams(vmem_limit_bytes=8 * 2**20),
        name="finish",
    )(feats, gram)


def on_device(snapshots, basis, neighbour_ids):
    feats, gram = exchange_call(snapshots[0], basis[0].T, neighbour_ids.T)
    return finish_call(feats, gram)[None]


def solution(mesh):
    return jax.shard_map(
        on_device,
        mesh=mesh,
        in_specs=(P("tm", "row", None), P("tm", "row", None), P()),
        out_specs=P("tm", "row", None),
        check_vma=False,
    )
```

```python
import jax
import jax.numpy as jnp
import numpy as np
from jax import lax
from jax.experimental import pallas as pl
from jax.experimental.pallas import tpu as pltpu
from jax.sharding import PartitionSpec as P

MESH = pl.DeviceIdType.MESH
BF = jnp.bfloat16
F32 = jnp.float32
RANK = 64
TIME = 2048
EPS = 1e-6
PAIRS = [(i, j) for i in range(RANK) for j in range(i, RANK)]
ROWS = 568
COLS = 2272
PAD = 8
HEAD = 256
NT = (((1,), (1,)), ((), ()))


def place():
    t = lax.axis_index("tm")
    return lax.axis_index("row"), lax.div(t, 8), lax.rem(lax.div(t, 2), 4), lax.rem(t, 2)


def at(x, z, y, c):
    return (lax.rem(x, 4), (lax.rem(z, 8) * 4 + lax.rem(y, 4)) * 2 + lax.rem(c, 2))


def remote(src, dst, ss, rs, dev):
    return pltpu.make_async_remote_copy(
        src_ref=src, dst_ref=dst, send_sem=ss, recv_sem=rs, device_id=dev, device_id_type=MESH
    )


def scale_of(blocks):
    energy = None
    for v in blocks:
        e = jnp.sum(v * v, axis=1, keepdims=True)
        energy = e if energy is None else energy + e
    return lax.rsqrt(energy / TIME + EPS)


def quad_tile(nf, chunk, first, line):
    out, q = None, first
    while q < first + 8:
        i, j = PAIRS[q]
        b = q - first
        val = nf[chunk, pl.ds(PAD + i, 1), :] * nf[chunk, pl.ds(PAD + j - b, 8), :]
        out = val if out is None else jnp.where(line < b, out, val)
        q += min(RANK - j, first + 8 - q)
    return out


def build_quads(nf, feats, first, last):
    line = lax.broadcasted_iota(jnp.int32, (8, 128), 0)

    def one(chunk, carry):
        col = pl.ds(pl.multiple_of(chunk * 128, 128), 128)
        for t in range(0, len(PAIRS), 16):
            pair = [quad_tile(nf, chunk, t, line), quad_tile(nf, chunk, t + 8, line)]
            feats[192 + t : 208 + t, col] = jnp.concatenate(pair, 0).astype(BF)
        return carry

    lax.fori_loop(first, last, one, 0)


def exchange(snap, basis, ids_hbm, feats, gram,
             sv, bv, ids, psend, precv, own, raw, nf, gy, gz, zsend, zrecv, mix, msend, ysend, yrecv, n1, n2,
             ld, ps, pr, os, orr, ys, yr, cs, cr, gs, gr, ns, nr, n1s, n1r, zs, zr, ms, mr, qs, qr, n2s, n2r):
    x, z, y, c = place()
    s = lax.axis_index("tm")
    me = y * 2 + c
    s_next = (x, lax.rem(s + 1, 64))
    s_prev = (x, lax.rem(s + 63, 64))

    def cols(q):
        return pl.ds(pl.multiple_of(q * 512, 512), 512)

    order = (2, 1, 3, 0)
    quarter = [lax.rem(x + k, 4) for k in order]
    fetch = [pltpu.make_async_copy(basis, bv, ld.at[4]), pltpu.make_async_copy(ids_hbm, ids, ld.at[5])]
    loads = [pltpu.make_async_copy(snap.at[:, cols(q)], sv.at[:, cols(q)], ld.at[i]) for i, q in enumerate(quarter)]
    fetch[0].start()
    for cp in loads:
        cp.start()
    fetch[1].start()

    bar = pltpu.get_barrier_semaphore()
    peers = [at(x + k, z, y, c) for k in (1, 2, 3)] + [at(x, z, y + k, c) for k in (1, 2, 3)]
    peers += [at(x, z + k, y, c) for k in range(1, 8)] + [at(x, z, y, c + 1), s_next, s_prev]
    for p in peers:
        pl.semaphore_signal(bar, inc=1, device_id=p, device_id_type=MESH)

    def project(i):
        loads[i].wait()
        return jnp.dot(bv[...], sv[:, cols(quarter[i])], preferred_element_type=F32)

    fetch[0].wait()
    sums = []
    for i, k in enumerate(order[:3]):
        psend[i] = project(i).astype(BF)
        if i == 0:
            pl.semaphore_wait(bar, len(peers))
        cp = remote(psend.at[i], precv.at[i], ps.at[i], pr.at[i], at(x + k, z, y, c))
        cp.start()
        sums.append(cp)
    total = project(3)
    fetch[1].wait()
    feats[64:192, :] = jnp.zeros((128, TIME), BF)
    feats[COLS:, :] = jnp.zeros((feats.shape[0] - COLS, TIME), BF)
    nf[:, 0:PAD, :] = jnp.zeros((16, PAD, 128), F32)
    nf[:, PAD + RANK :, :] = jnp.zeros((16, 8, 128), F32)
    for i in range(3):
        sums[i].wait_recv()
        total = total + precv[i].astype(F32)

    own[x] = total
    low = total.astype(BF)
    gy[me] = low[:, :256]
    gz[z] = low[:, 256:]
    raw[...] = low
    ycp = {}
    for k in (2, 1, 3):
        ycp[k] = remote(gy.at[me], gy.at[me], ys.at[k - 1], yr.at[k - 1], at(x, z, y + k, c))
        ycp[k].start()
    ccp = [remote(gy.at[me], gy.at[me], cs.at[0], cr.at[0], at(x, z, y, c + 1))]
    ccp[0].start()
    gcp = {}
    for k in (4, 3, 5, 2, 6, 1, 7):
        gcp[k] = remote(gz.at[z], gz.at[z], gs.at[k - 1], gr.at[k - 1], at(x, z + k, y, c))
        gcp[k].start()
    ncp = remote(raw, n1.at[x], ns.at[0], nr.at[0], s_next)
    ncp.start()
    ocp = []
    for k in (2, 1, 3):
        cp = remote(own.at[x], own.at[x], os.at[k - 1], orr.at[k - 1], at(x + k, z, y, c))
        cp.start()
        ocp.append(cp)

    for k in (1, 3, 2):
        ycp[k].wait_recv()
        slot = lax.rem(y + 4 - k, 4) * 2 + c
        cp = remote(gy.at[slot], gy.at[slot], cs.at[k], cr.at[k], at(x, z, y, c + 1))
        cp.start()
        ccp.append(cp)
    for cp in ccp:
        cp.wait_recv()
    want = ids[1, s]
    zcp = {}
    for k in (4, 3, 5, 2, 6, 1, 7):
        asked = ids[1, (lax.rem(z + k, 8) * 4 + y) * 2 + c]
        zsend[k - 1] = gy[lax.rem(asked, 8)]
        zcp[k] = remote(zsend.at[k - 1], zrecv.at[z], zs.at[k - 1], zr.at[k - 1], at(x, z + k, y, c))
        zcp[k].start()
    zrecv[z] = gy[lax.rem(want, 8)]

    for cp in ocp:
        cp.wait_recv()
    scale = scale_of([own[r] for r in range(4)])
    for r in range(4):
        n = (own[r] * scale).astype(BF)
        feats[0:64, 512 * r : 512 * r + 512] = n
        wide = n.astype(F32)
        for k in range(4):
            nf[4 * r + k, pl.ds(PAD, RANK), :] = wide[:, 128 * k : 128 * k + 128]

    def neighbour(ref, row):
        blocks = [ref[r].astype(F32) for r in range(4)]
        scale = scale_of(blocks)
        for r in range(4):
            feats[row : row + 64, 512 * r : 512 * r + 512] = (blocks[r] * scale).astype(BF)


    lines = pl.ds(pl.multiple_of(lax.div(x * ROWS, 16) * 16, 16), 576)
    spans = [(k, min(k + 256, COLS)) for k in range(HEAD, COLS, 256)]

    def multiply(first, last):
        for lo, hi in spans[first:last]:
            block = lax.dot_general(feats[lines, :], feats[lo : lo + 256, :], NT, preferred_element_type=F32)
            gram[:, lo - HEAD : hi - HEAD] = block[:, : hi - lo] * (1.0 / TIME)

    for k in (1, 7, 2, 6, 3, 5, 4):
        gcp[k].wait_recv()
    for yy in range(4):
        msend[yy] = gz[lax.div(ids[1, (z * 4 + yy) * 2 + 1 - c], 8)]
    mcp = remote(msend, mix.at[c], ms.at[0], mr.at[0], at(x, z, y, c + 1))
    mcp.start()
    for yy in range(4):
        mix[c, yy] = gz[lax.div(ids[1, (z * 4 + yy) * 2 + c], 8)]

    ncp.wait_recv()
    n1cp = []
    for k in (2, 1, 3):
        cp = remote(n1.at[x], n1.at[x], n1s.at[k - 1], n1r.at[k - 1], at(x + k, z, y, c))
        cp.start()
        n1cp.append(cp)
    build_quads(nf, feats, 0, 6)

    mcp.wait_recv()
    qcp = []
    for k in (2, 1, 3):
        yy = lax.rem(y + k, 4)
        asked = ids[1, (z * 4 + yy) * 2 + c]
        ysend[k - 1] = mix[lax.rem(asked, 2), yy]
        cp = remote(ysend.at[k - 1], yrecv.at[y], qs.at[k - 1], qr.at[k - 1], at(x, z, y + k, c))
        cp.start()
        qcp.append(cp)
    yrecv[y] = mix[lax.rem(want, 2), y]

    build_quads(nf, feats, 6, 16)
    n2cp = []

    def share(h):
        for k in (2, 1, 3):
            sem = 3 * h + k - 1
            cp = remote(n2.at[h, x], n2.at[h, x], n2s.at[sem], n2r.at[sem], at(x + k, z, y, c))
            cp.start()
            n2cp.append(cp)

    for cp in qcp:
        cp.wait_recv()
    n2[1, x] = yrecv[lax.div(lax.rem(want, 8), 2)]
    share(1)
    for k in (1, 7, 2, 6, 3, 5, 4):
        zcp[k].wait_recv()
    n2[0, x] = zrecv[lax.div(want, 8)]
    share(0)

    multiply(0, 8)

    for cp in n1cp:
        cp.wait_recv()
    neighbour(n1, 64)
    for cp in n2cp:
        cp.wait_recv()
    halves = [n2[h, r].astype(F32) for r in range(4) for h in range(2)]
    scale = scale_of(halves)
    for r in range(8):
        feats[128:192, 256 * r : 256 * r + 256] = (halves[r] * scale).astype(BF)
    for cp in sums + list(ycp.values()) + ccp + list(gcp.values()) + [ncp] + ocp + n1cp + list(zcp.values()) + [mcp] + qcp + n2cp:
        cp.wait_send()


def exchange_call(snap, basis, ids):
    vm = pl.BlockSpec(memory_space=pltpu.VMEM)
    hbm = pl.BlockSpec(memory_space=pltpu.HBM)
    dma = pltpu.SemaphoreType.DMA
    half = (64, 256)
    full = (64, 512)
    sems = [6, 3, 3, 3, 3, 3, 3, 4, 4, 7, 7, 1, 1, 3, 3, 7, 7, 1, 1, 3, 3, 6, 6]
    bufs = [(512, 2048), (64, 512), None, (3,) + full, (3,) + full, (4,) + full, full, (16, PAD + RANK + 8, 128),
            (8,) + half, (8,) + half, (7,) + half, (8,) + half, (2, 4) + half, (4,) + half, (3,) + half, (4,) + half,
            (4,) + full, (2, 4) + half]
    wide = (5, 7)
    scratch = [pltpu.SMEM((2, 64), jnp.int32) if b is None else pltpu.VMEM(b, F32 if i in wide else BF) for i, b in enumerate(bufs)]
    return pl.pallas_call(
        exchange,
        out_shape=[jax.ShapeDtypeStruct((2304, TIME), BF), jax.ShapeDtypeStruct((576, COLS - HEAD), F32)],
        in_specs=[hbm] * 3,
        out_specs=[vm] * 2,
        scratch_shapes=scratch + [dma((n,)) for n in sems],
        compiler_params=pltpu.CompilerParams(collective_id=0, has_side_effects=True, vmem_limit_bytes=24 * 2**20),
        name="exchange",
    )(snap, basis, ids)


def finish(feats, gram, out, head, band, sem):
    x = lax.axis_index("row")
    off = pl.multiple_of(lax.rem(x, 2) * 8, 8)

    def ship(src, lo, size, n):
        return pltpu.make_async_copy(src, out.at[pl.ds(lo, size), pl.ds(HEAD, COLS - HEAD)], sem.at[n])

    early = [ship(gram.at[pl.ds(off + lo, size), :], lo, size, n) for n, (lo, size) in enumerate([(192, 184), (376, 192), (0, 64)])]
    middle = ship(gram.at[pl.ds(off + 64, 128), :], 64, 128, 3)
    late = ship(band, 64, 128, 3)
    for cp in early:
        cp.start()

    @pl.when(x != 0)
    def _():
        middle.start()

    lines = pl.ds(pl.multiple_of(lax.div(x * ROWS, 16) * 16, 16), 576)
    head[...] = lax.dot_general(feats[lines, :], feats[0:HEAD, :], NT, preferred_element_type=F32) * (1.0 / TIME)
    first = pltpu.make_async_copy(head.at[pl.ds(off, ROWS), :], out.at[:, pl.ds(0, HEAD)], sem.at[4])
    first.start()

    @pl.when(x == 0)
    def _():
        for lo in range(HEAD, COLS, 768):
            hi = min(lo + 768, COLS)
            block = lax.dot_general(feats[64:192, :], feats[lo : lo + 768, :], NT, preferred_element_type=F32)
            band[:, lo - HEAD : hi - HEAD] = block[:, : hi - lo] * (1.0 / TIME)
        late.start()

    for cp in early + [middle, first]:
        cp.wait()


def finish_call(feats, gram):
    vm = pl.BlockSpec(memory_space=pltpu.VMEM)
    return pl.pallas_call(
        finish,
        out_shape=jax.ShapeDtypeStruct((ROWS, COLS), F32),
        in_specs=[vm] * 2,
        out_specs=pl.BlockSpec(memory_space=pltpu.HBM),
        scratch_shapes=[pltpu.VMEM((576, HEAD), F32), pltpu.VMEM((128, COLS - HEAD), F32), pltpu.SemaphoreType.DMA((5,))],
        compiler_params=pltpu.CompilerParams(vmem_limit_bytes=8 * 2**20),
        name="finish",
    )(feats, gram)


def on_device(snapshots, basis, neighbour_ids):
    operands = [pltpu.with_memory_space_constraint(a, pltpu.HBM) for a in (snapshots[0], basis[0].T, neighbour_ids.T)]
    feats, gram = exchange_call(*operands)
    return finish_call(feats, gram)[None]


def solution(mesh):
    return jax.shard_map(
        on_device,
        mesh=mesh,
        in_specs=(P("tm", "row", None), P("tm", "row", None), P()),
        out_specs=P("tm", "row", None),
        check_vma=False,
    )
```

```python
import jax
import jax.numpy as jnp
import numpy as np
from jax import lax
from jax.experimental import pallas as pl
from jax.experimental.pallas import tpu as pltpu
from jax.sharding import PartitionSpec as P

MESH = pl.DeviceIdType.MESH
BF = jnp.bfloat16
F32 = jnp.float32
RANK = 64
TIME = 2048
EPS = 1e-6
PAIRS = [(i, j) for i in range(RANK) for j in range(i, RANK)]
ROWS = 568
COLS = 2272
PAD = 8
HEAD = 256
NT = (((1,), (1,)), ((), ()))


def place():
    t = lax.axis_index("tm")
    return lax.axis_index("row"), lax.div(t, 8), lax.rem(lax.div(t, 2), 4), lax.rem(t, 2)


def at(x, z, y, c):
    return (lax.rem(x, 4), (lax.rem(z, 8) * 4 + lax.rem(y, 4)) * 2 + lax.rem(c, 2))


def remote(src, dst, ss, rs, dev):
    return pltpu.make_async_remote_copy(
        src_ref=src, dst_ref=dst, send_sem=ss, recv_sem=rs, device_id=dev, device_id_type=MESH
    )


def scale_of(blocks):
    energy = None
    for v in blocks:
        e = jnp.sum(v * v, axis=1, keepdims=True)
        energy = e if energy is None else energy + e
    return lax.rsqrt(energy / TIME + EPS)


def quad_tile(nf, chunk, first, line):
    out, q = None, first
    while q < first + 8:
        i, j = PAIRS[q]
        b = q - first
        val = nf[chunk, pl.ds(PAD + i, 1), :] * nf[chunk, pl.ds(PAD + j - b, 8), :]
        out = val if out is None else jnp.where(line < b, out, val)
        q += min(RANK - j, first + 8 - q)
    return out


def build_quads(nf, feats, first, last):
    line = lax.broadcasted_iota(jnp.int32, (8, 128), 0)

    def one(chunk, carry):
        col = pl.ds(pl.multiple_of(chunk * 128, 128), 128)
        for t in range(0, len(PAIRS), 16):
            pair = [quad_tile(nf, chunk, t, line), quad_tile(nf, chunk, t + 8, line)]
            feats[192 + t : 208 + t, col] = jnp.concatenate(pair, 0).astype(BF)
        return carry

    lax.fori_loop(first, last, one, 0)


def exchange(snap, basis, ids_hbm, feats, gram,
             sv, bv, ids, psend, precv, own, raw, nf, gy, gz, zsend, zrecv, mix, msend, ysend, yrecv, n1, n2,
             ld, ps, pr, os, orr, ys, yr, cs, cr, gs, gr, ns, nr, n1s, n1r, zs, zr, ms, mr, qs, qr, n2s, n2r):
    x, z, y, c = place()
    s = lax.axis_index("tm")
    me = y * 2 + c
    s_next = (x, lax.rem(s + 1, 64))
    s_prev = (x, lax.rem(s + 63, 64))

    def cols(q):
        return pl.ds(pl.multiple_of(q * 512, 512), 512)

    order = (2, 1, 3, 0)
    quarter = [lax.rem(x + k, 4) for k in order]
    fetch = [pltpu.make_async_copy(basis, bv, ld.at[4]), pltpu.make_async_copy(ids_hbm, ids, ld.at[5])]
    loads = [pltpu.make_async_copy(snap.at[:, cols(q)], sv.at[:, cols(q)], ld.at[i]) for i, q in enumerate(quarter)]
    fetch[0].start()
    for cp in loads:
        cp.start()
    fetch[1].start()

    bar = pltpu.get_barrier_semaphore()
    peers = [at(x + k, z, y, c) for k in (1, 2, 3)] + [at(x, z, y + k, c) for k in (1, 2, 3)]
    peers += [at(x, z + k, y, c) for k in range(1, 8)] + [at(x, z, y, c + 1), s_next, s_prev]
    for p in peers:
        pl.semaphore_signal(bar, inc=1, device_id=p, device_id_type=MESH)

    def project(i):
        loads[i].wait()
        return jnp.dot(bv[...], sv[:, cols(quarter[i])], preferred_element_type=F32)

    fetch[0].wait()
    sums = {}

    def give(i, h):
        part = pl.ds(256 * h, 256)
        sums[i, h] = remote(psend.at[i, :, part], precv.at[i, :, part], ps.at[2 * i + h], pr.at[2 * i + h], at(x + order[i], z, y, c))
        sums[i, h].start()

    for i in range(3):
        psend[i] = project(i).astype(BF)
        if i == 0:
            pl.semaphore_wait(bar, len(peers))
        give(i, 0)
    for i in range(3):
        give(i, 1)
    total = project(3)
    fetch[1].wait()
    feats[64:192, :] = jnp.zeros((128, TIME), BF)
    feats[COLS:, :] = jnp.zeros((feats.shape[0] - COLS, TIME), BF)
    nf[:, 0:PAD, :] = jnp.zeros((16, PAD, 128), F32)
    nf[:, PAD + RANK :, :] = jnp.zeros((16, 8, 128), F32)
    lower = total[:, :256]
    for i in range(3):
        sums[i, 0].wait_recv()
        lower = lower + precv[i, :, :256].astype(F32)
    gy[me] = lower.astype(BF)
    ycp = [remote(gy.at[me], gy.at[me], ys.at[i], yr.at[i], at(x, z, y + k, c)) for i, k in enumerate((2, 1, 3))]
    ccp = [remote(gy.at[me], gy.at[me], cs.at[3], cr.at[3], at(x, z, y, c + 1))]
    for cp in ycp + ccp:
        cp.start()
    upper = total[:, 256:]
    for i in range(3):
        sums[i, 1].wait_recv()
        upper = upper + precv[i, :, 256:].astype(F32)
    gz[z] = upper.astype(BF)
    gcp = [remote(gz.at[z], gz.at[z], gs.at[k - 1], gr.at[k - 1], at(x, z + k, y, c)) for k in (4, 3, 5, 2, 6, 1, 7)]
    for cp in gcp:
        cp.start()
    own[x, :, :256] = lower
    own[x, :, 256:] = upper
    raw[:, :256] = lower.astype(BF)
    raw[:, 256:] = upper.astype(BF)
    ncp = remote(raw, n1.at[x], ns.at[0], nr.at[0], s_next)
    ocp = [remote(own.at[x], own.at[x], os.at[i], orr.at[i], at(x + k, z, y, c)) for i, k in enumerate((2, 1, 3))]
    for cp in ocp + [ncp]:
        cp.start()

    for i, k in ((1, 1), (2, 3), (0, 2)):
        ycp[i].wait_recv()
        slot = lax.rem(y + 4 - k, 4) * 2 + c
        cp = remote(gy.at[slot], gy.at[slot], cs.at[i], cr.at[i], at(x, z, y, c + 1))
        cp.start()
        ccp.append(cp)
    for cp in ccp:
        cp.wait_recv()
    want = ids[1, s]
    zcp = {}
    for k in (4, 3, 5, 2, 6, 1, 7):
        asked = ids[1, (lax.rem(z + k, 8) * 4 + y) * 2 + c]
        zsend[k - 1] = gy[lax.rem(asked, 8)]
        zcp[k] = remote(zsend.at[k - 1], zrecv.at[z], zs.at[k - 1], zr.at[k - 1], at(x, z + k, y, c))
        zcp[k].start()
    zrecv[z] = gy[lax.rem(want, 8)]

    for cp in ocp:
        cp.wait_recv()
    scale = scale_of([own[r] for r in range(4)])
    for r in range(4):
        n = (own[r] * scale).astype(BF)
        feats[0:64, 512 * r : 512 * r + 512] = n
        wide = n.astype(F32)
        for k in range(4):
            nf[4 * r + k, pl.ds(PAD, RANK), :] = wide[:, 128 * k : 128 * k + 128]

    def neighbour(ref, row):
        blocks = [ref[r].astype(F32) for r in range(4)]
        scale = scale_of(blocks)
        for r in range(4):
            feats[row : row + 64, 512 * r : 512 * r + 512] = (blocks[r] * scale).astype(BF)


    lines = pl.ds(pl.multiple_of(lax.div(x * ROWS, 16) * 16, 16), 576)
    spans = [(k, min(k + 256, COLS)) for k in range(HEAD, COLS, 256)]

    def multiply(first, last):
        @pl.when(x == 0)
        def _():
            for lo, hi in spans[first:last]:
                left = jnp.concatenate([feats[0:64, :], feats[192:576, :]], 0)
                block = lax.dot_general(left, feats[lo : lo + 256, :], NT, preferred_element_type=F32)[:, : hi - lo] * (1.0 / TIME)
                gram[0:64, lo - HEAD : hi - HEAD] = block[0:64]
                gram[192:576, lo - HEAD : hi - HEAD] = block[64:]

        @pl.when(x != 0)
        def _():
            for lo, hi in spans[first:last]:
                block = lax.dot_general(feats[lines, :], feats[lo : lo + 256, :], NT, preferred_element_type=F32)
                gram[:, lo - HEAD : hi - HEAD] = block[:, : hi - lo] * (1.0 / TIME)

    for cp in gcp:
        cp.wait_recv()
    for yy in range(4):
        msend[yy] = gz[lax.div(ids[1, (z * 4 + yy) * 2 + 1 - c], 8)]
    mcp = remote(msend, mix.at[c], ms.at[0], mr.at[0], at(x, z, y, c + 1))
    mcp.start()
    for yy in range(4):
        mix[c, yy] = gz[lax.div(ids[1, (z * 4 + yy) * 2 + c], 8)]

    ncp.wait_recv()
    n1cp = []
    for k in (2, 1, 3):
        cp = remote(n1.at[x], n1.at[x], n1s.at[k - 1], n1r.at[k - 1], at(x + k, z, y, c))
        cp.start()
        n1cp.append(cp)
    build_quads(nf, feats, 0, 6)

    mcp.wait_recv()
    qcp = []
    for k in (2, 1, 3):
        yy = lax.rem(y + k, 4)
        asked = ids[1, (z * 4 + yy) * 2 + c]
        ysend[k - 1] = mix[lax.rem(asked, 2), yy]
        cp = remote(ysend.at[k - 1], yrecv.at[y], qs.at[k - 1], qr.at[k - 1], at(x, z, y + k, c))
        cp.start()
        qcp.append(cp)
    yrecv[y] = mix[lax.rem(want, 2), y]

    build_quads(nf, feats, 6, 16)
    n2cp = []

    def share(h):
        for k in (2, 1, 3):
            sem = 3 * h + k - 1
            cp = remote(n2.at[h, x], n2.at[h, x], n2s.at[sem], n2r.at[sem], at(x + k, z, y, c))
            cp.start()
            n2cp.append(cp)

    for cp in qcp:
        cp.wait_recv()
    n2[1, x] = yrecv[lax.div(lax.rem(want, 8), 2)]
    share(1)
    for k in (1, 7, 2, 6, 3, 5, 4):
        zcp[k].wait_recv()
    n2[0, x] = zrecv[lax.div(want, 8)]
    share(0)

    multiply(0, 8)

    for cp in n1cp:
        cp.wait_recv()
    neighbour(n1, 64)
    for cp in n2cp:
        cp.wait_recv()
    halves = [n2[h, r].astype(F32) for r in range(4) for h in range(2)]
    scale = scale_of(halves)
    for r in range(8):
        feats[128:192, 256 * r : 256 * r + 256] = (halves[r] * scale).astype(BF)
    for cp in list(sums.values()) + ycp + ccp + gcp + [ncp] + ocp + n1cp + list(zcp.values()) + [mcp] + qcp + n2cp:
        cp.wait_send()


def exchange_call(snap, basis, ids):
    vm = pl.BlockSpec(memory_space=pltpu.VMEM)
    hbm = pl.BlockSpec(memory_space=pltpu.HBM)
    dma = pltpu.SemaphoreType.DMA
    half = (64, 256)
    full = (64, 512)
    sems = [6, 6, 6, 3, 3, 3, 3, 4, 4, 7, 7, 1, 1, 3, 3, 7, 7, 1, 1, 3, 3, 6, 6]
    bufs = [(512, 2048), (64, 512), None, (3,) + full, (3,) + full, (4,) + full, full, (16, PAD + RANK + 8, 128),
            (8,) + half, (8,) + half, (7,) + half, (8,) + half, (2, 4) + half, (4,) + half, (3,) + half, (4,) + half,
            (4,) + full, (2, 4) + half]
    wide = (5, 7)
    scratch = [pltpu.SMEM((2, 64), jnp.int32) if b is None else pltpu.VMEM(b, F32 if i in wide else BF) for i, b in enumerate(bufs)]
    return pl.pallas_call(
        exchange,
        out_shape=[jax.ShapeDtypeStruct((2304, TIME), BF), jax.ShapeDtypeStruct((576, COLS - HEAD), F32)],
        in_specs=[hbm] * 3,
        out_specs=[vm] * 2,
        scratch_shapes=scratch + [dma((n,)) for n in sems],
        compiler_params=pltpu.CompilerParams(collective_id=0, has_side_effects=True, vmem_limit_bytes=24 * 2**20),
        name="exchange",
    )(snap, basis, ids)


def finish(feats, gram, out, head, band, sem):
    x = lax.axis_index("row")
    off = pl.multiple_of(lax.rem(x, 2) * 8, 8)

    def ship(src, lo, size, n):
        return pltpu.make_async_copy(src, out.at[pl.ds(lo, size), pl.ds(HEAD, COLS - HEAD)], sem.at[n])

    early = [ship(gram.at[pl.ds(off + lo, size), :], lo, size, n) for n, (lo, size) in enumerate([(192, 184), (376, 192), (0, 64)])]
    middle = ship(gram.at[pl.ds(off + 64, 128), :], 64, 128, 3)
    for cp in early:
        cp.start()

    @pl.when(x != 0)
    def _():
        middle.start()

    lines = pl.ds(pl.multiple_of(lax.div(x * ROWS, 16) * 16, 16), 576)
    head[...] = lax.dot_general(feats[lines, :], feats[0:HEAD, :], NT, preferred_element_type=F32) * (1.0 / TIME)
    first = pltpu.make_async_copy(head.at[pl.ds(off, ROWS), :], out.at[:, pl.ds(0, HEAD)], sem.at[4])
    first.start()

    late = []
    for n, lo in enumerate(range(HEAD, COLS, 768)):
        size = min(768, COLS - lo)
        late.append(pltpu.make_async_copy(band.at[:, pl.ds(lo - HEAD, size)], out.at[pl.ds(64, 128), pl.ds(lo, size)], sem.at[5 + n]))

    @pl.when(x == 0)
    def _():
        for cp, lo in zip(late, range(HEAD, COLS, 768)):
            hi = min(lo + 768, COLS)
            block = lax.dot_general(feats[64:192, :], feats[lo : lo + 768, :], NT, preferred_element_type=F32)
            band[:, lo - HEAD : hi - HEAD] = block[:, : hi - lo] * (1.0 / TIME)
            cp.start()

    for cp in early + [first]:
        cp.wait()

    @pl.when(x != 0)
    def _():
        middle.wait()

    @pl.when(x == 0)
    def _():
        for cp in late:
            cp.wait()


def finish_call(feats, gram):
    vm = pl.BlockSpec(memory_space=pltpu.VMEM)
    return pl.pallas_call(
        finish,
        out_shape=jax.ShapeDtypeStruct((ROWS, COLS), F32),
        in_specs=[vm] * 2,
        out_specs=pl.BlockSpec(memory_space=pltpu.HBM),
        scratch_shapes=[pltpu.VMEM((576, HEAD), F32), pltpu.VMEM((128, COLS - HEAD), F32), pltpu.SemaphoreType.DMA((8,))],
        compiler_params=pltpu.CompilerParams(vmem_limit_bytes=8 * 2**20),
        name="finish",
    )(feats, gram)


def on_device(snapshots, basis, neighbour_ids):
    operands = [pltpu.with_memory_space_constraint(a, pltpu.HBM) for a in (snapshots[0], basis[0].T, neighbour_ids.T)]
    feats, gram = exchange_call(*operands)
    return finish_call(feats, gram)[None]


def solution(mesh):
    return jax.shard_map(
        on_device,
        mesh=mesh,
        in_specs=(P("tm", "row", None), P("tm", "row", None), P()),
        out_specs=P("tm", "row", None),
        check_vma=False,
    )
```
